32 devices in a mesh: dp: 4 (over z), table: 8 (over y, x, core).
Axes of the slice: x: 2, y: 2, z: 4, core: 2. Of those that a mesh axis runs over, the one named last changes fastest.
Arguments:
- table: bfloat16 [32768, 512], P('table'), may hold values from -6 to 6
- w_in: bfloat16 [512, 2048], replicated, may hold values from -0.25 to 0.25
- w_out: bfloat16 [512, 512], replicated, may hold values from -0.25 to 0.25
- owner: int32 [32768, 2], P(('dp', 'table')), may hold values from 0 to 7, all different within a row; in each aligned block of 1024 rows (0 to 1023, 1024 to 2047, ...) at most 512 rows name the same one
- local_row: int32 [32768, 2], P(('dp', 'table')), may hold values from 0 to 4095
- doc_ids: int32 [32, 1024], P(('dp', 'table')), may hold values from 0 to 3, never falling along the last dimension, each value on 1 to 768 neighbouring positions
- out_grad: bfloat16 [32768, 512], P(('dp', 'table')), may hold values from -6 to 6
Outputs:
- layer_out: bfloat16 [32768, 512], P(('dp', 'table'))
- grad_w_in: float32 [512, 2048], replicated
- grad_w_out: float32 [512, 512], replicated
- grad_table: float32 [32768, 512], P('table', 'dp')
The draws below stay inside these ranges and needn't reach their ends.
Inputs may be any that keep to these rules, and one draw needn't show every extreme that they name: The 2 owners of one event differ; among the events of one block of 1024, no owner is named by more than 512 lookups. `doc_ids`: along a row the ids never fall; every id of 0 to 3 covers 1 to 768 events.
All inputs are finite; a program needn't handle non-finite values.
Results may differ from the reference program's by a relative error of at most 0.014.
Values may be sent and summed in bfloat16 or wider, within the bound.
A program may use at most 128 MiB of HBM per device.

```python
import math
import jax
import jax.numpy as jnp
import numpy as np
from jax import lax

D = 512
HEADS = 4
NTAB = 2
TOK_DEV = 1024
SEQ_DEV = 4
MAXLEN = 768
ROWS_DEV = 4096
CAP = 512
ROWS = 32768
NBLOCK = 32
TOKENS = 32768
N_TABLE = 8


def with_ends(entries, key, least, largest):
    shape = entries.shape
    place = [jax.random.randint(jax.random.fold_in(key, axis), (), 0, shape[axis]) for axis in range(len(shape))]
    entries = entries.at[tuple(place)].set(least)
    longest = shape.index(max(shape))
    place[longest] = (place[longest] + 1) % shape[longest]
    return entries.at[tuple(place)].set(largest)


def shard_levels(stream_key, dims, pieces, least, largest):
    def one(axis_at, parts):
        steps = jax.random.uniform(jax.random.fold_in(jax.random.fold_in(stream_key, 6), axis_at), (parts,), jnp.float32, least / len(pieces), largest / len(pieces))
        return jnp.repeat(jnp.exp(steps), dims[axis_at] // parts).reshape((-1,) + (1,) * (len(dims) - axis_at - 1))

    factor_of = one(*pieces[0])
    for cut in pieces[1:]:
        factor_of = factor_of * one(*cut)
    return factor_of


def profile(amount, total, reach, skew):
    portions = [(1 << 20) // math.isqrt(rank ** skew) + 1 for rank in range(2, amount + 1)]
    rest, given = total - reach - (amount - 1), [1] * (amount - 1)
    while rest > 0:
        movable = [i for i in range(amount - 1) if given[i] < reach]
        whole, remaining = sum([portions[i] for i in movable]), rest
        for i in movable:
            extra = min(reach - given[i], max(1, remaining * portions[i] // whole), rest)
            given[i] = given[i] + extra
            rest = rest - extra
    return np.array([reach] + given)


def ragged_sizes(key, number_of, total, limit, skew):
    if number_of == 2:
        one = jax.random.randint(key, (), max(1, total - limit), min(limit, total - 1) + 1)
        return jnp.stack([one, total - one])
    sizes = jnp.asarray(profile(number_of, total, limit, skew), jnp.int32)
    twos = (number_of - 1) // 2
    giver, receiver = sizes[1:1 + 2 * twos:2], sizes[2:2 + 2 * twos:2]
    slack = jnp.minimum(giver - 1, limit - receiver)
    shifted = jax.random.randint(jax.random.fold_in(key, 1), (twos,), 0, 1 << 20) % (slack + 1)
    sizes = sizes.at[1:1 + 2 * twos:2].set(giver - shifted).at[2:2 + 2 * twos:2].set(receiver + shifted)
    return sizes[jax.random.permutation(jax.random.fold_in(key, 2), number_of)]


def shared_out(key, own, number, rows, number_of, top, reach, lean):
    sequence = jax.random.permutation(key, number_of)
    crowded, ordinary = portions_of(number_of, rows * top, reach, lean, True), portions_of(number_of, rows * top, reach, lean, False)
    places = jnp.arange(number_of)

    def named(sizes, turn):
        used = int((sizes > 0).sum())
        fixed = max(1, used // 4)
        moved = fixed + (places - fixed + turn * (used - fixed)) % max(1, number_of - fixed)
        return jnp.zeros((number_of,), jnp.int32).at[sequence[jnp.where(places < fixed, places, moved)]].set(jnp.asarray(sizes, jnp.int32))

    sizes = jnp.where(number % 4 == 0, named(crowded, number // 4), named(ordinary, number - number // 4 - 1))
    mixed = jax.random.permutation(jax.random.fold_in(own, 3), number_of)
    giver, sink = mixed[0:number_of // 2 * 2:2], mixed[1:number_of // 2 * 2:2]
    slack = jnp.minimum(sizes[giver] - 1, reach - sizes[sink]) // 2
    slack = jnp.where((giver == sequence[0]) | (sink == sequence[0]) | (sizes[sink] == 0), 0, jnp.maximum(slack, 0))
    moved = jax.random.randint(jax.random.fold_in(own, 4), (number_of // 2,), 0, 1 << 20) % (slack + 1)
    sizes = sizes.at[giver].add(-moved).at[sink].add(moved)
    labels = jnp.searchsorted(jnp.cumsum(sizes), jnp.arange(rows * top), side="right").astype(jnp.int32)
    listing = labels.reshape(top, rows).T
    listing = listing[jax.random.permutation(jax.random.fold_in(own, 1), rows)]
    turn = jax.random.randint(jax.random.fold_in(own, 2), (rows, 1), 0, top)
    return jnp.take_along_axis(listing, (jnp.arange(top)[None, :] + turn) % top, axis=1)


def portions_of(number_of, total, reach, lean, full):
    weights = [(1 << 20) // math.isqrt(grade ** lean) + 1 for grade in range(1, number_of + 1)]
    largest = reach if full else min(reach, max(-(-total // number_of), total * weights[0] // sum(weights)))
    least = 1 if total - largest >= number_of - 1 else 0
    counts, rest = [largest] + [least] * (number_of - 1), total - largest - least * (number_of - 1)
    while rest > 0:
        free = [i for i in range(1, number_of) if counts[i] < largest] or [i for i in range(1, number_of) if counts[i] < reach]
        mass, budget = sum([weights[i] for i in free]), rest
        for i in free:
            extra = min(reach - counts[i], max(1, budget * weights[i] // mass), rest)
            counts[i] = counts[i] + extra
            rest = rest - extra
    return np.array(counts)


def noise(rng, dims, scale, bound, pieces=(), dtype=jnp.bfloat16):
    array = scale * jax.random.normal(rng, dims, jnp.float32)
    if pieces:
        array = array * shard_levels(rng, dims, pieces, -0.22, 0.18)
    return jnp.clip(array, -bound, bound).astype(dtype)


def setup_inputs(seed: int = 0) -> dict:
    seeds = jax.random.split(jax.random.key(seed), 8)
    table = noise(seeds[0], (ROWS, D), 1.0, 6.0, ((0, 8),))
    w_in = noise(seeds[1], (D, 4 * D), D ** -0.5, 0.25)
    w_out = noise(seeds[2], (D, D), D ** -0.5, 0.25)
    owner_keys = jax.random.split(jax.random.fold_in(seeds[3], 1), TOKENS // TOK_DEV)
    owner_turns = jax.random.permutation(jax.random.fold_in(seeds[3], 3), TOKENS // TOK_DEV)
    owner = jax.vmap(lambda own, number: shared_out(jax.random.fold_in(seeds[3], 2), own, number, TOK_DEV, N_TABLE, NTAB, CAP, 2))(owner_keys, owner_turns).reshape((TOKENS, NTAB))
    local_row = with_ends(jax.random.randint(seeds[4], (TOKENS, NTAB), 0, ROWS_DEV), jax.random.fold_in(seeds[4], 1), 0, ROWS_DEV - 1).astype(jnp.int32)
    doc_ids = jax.vmap(lambda own: jnp.searchsorted(jnp.cumsum(ragged_sizes(own, SEQ_DEV, TOK_DEV, MAXLEN, 2)), jnp.arange(TOK_DEV), side="right"))(jax.random.split(seeds[5], NBLOCK)).reshape((NBLOCK, TOK_DEV)).astype(jnp.int32)
    out_grad = noise(seeds[6], (TOKENS, D), 1.0, 6.0, ((0, 32),))
    return {"table": table, "w_in": w_in, "w_out": w_out, "owner": owner, "local_row": local_row, "doc_ids": doc_ids, "out_grad": out_grad}


def normalize(values):
    center = values - lax.optimization_barrier(jnp.mean(values, axis=-1, keepdims=True))
    spread = lax.optimization_barrier(jnp.mean(center * center, axis=-1, keepdims=True))
    return center * lax.rsqrt(spread + 1e-06)

def hstu_layer(inputs, w_in, w_out, segment):
    length, width = inputs.shape
    head_dim = width // HEADS
    widened = inputs.astype(jnp.float32)
    normed = normalize(widened).astype(jnp.bfloat16)
    projected = jax.nn.silu(jnp.dot(normed, w_in, preferred_element_type=jnp.float32)).astype(jnp.bfloat16)
    gate_part, value_part, query_part, key_part = jnp.split(projected, 4, axis=1)
    query_heads = query_part.reshape(length, HEADS, head_dim).astype(jnp.float32)
    key_heads = key_part.reshape(length, HEADS, head_dim).astype(jnp.float32)
    value_heads = value_part.reshape(length, HEADS, head_dim).astype(jnp.float32)
    scores = jnp.einsum('thd,shd->hts', query_heads, key_heads) * head_dim ** (-0.5)
    row_index = lax.broadcasted_iota(jnp.int32, (length, length), 0)
    col_index = lax.broadcasted_iota(jnp.int32, (length, length), 1)
    allowed = (segment[:, None] == segment[None, :]) & (row_index >= col_index)
    weights = (jnp.where(allowed[None], jax.nn.silu(scores), 0.0) / MAXLEN).astype(jnp.bfloat16)
    mixed = jnp.einsum('hts,shd->thd', weights.astype(jnp.float32), value_heads).reshape(length, width)
    gated = (normalize(mixed) * gate_part.astype(jnp.float32)).astype(jnp.bfloat16)
    return (widened + jnp.dot(gated, w_out, preferred_element_type=jnp.float32)).astype(jnp.bfloat16)

def reference(table, w_in, w_out, owner, local_row, doc_ids, out_grad):
    row_ids = (owner * ROWS_DEV + local_row).astype(jnp.int32)
    fetched = jnp.take(table, row_ids.reshape(-1), axis=0).astype(jnp.float32).reshape(TOKENS, NTAB, D)
    embedded = lax.optimization_barrier(jnp.sum(fetched, axis=1)).astype(jnp.bfloat16)
    blocks = embedded.reshape(NBLOCK, TOK_DEV, D)
    cotangents = out_grad.reshape(NBLOCK, TOK_DEV, D)

    def advance(carry, piece):
        block_in, block_seg, block_cot = piece

        def forward(first, second, third):
            return hstu_layer(first, second, third, block_seg)
        result, pullback = jax.vjp(forward, block_in, w_in, w_out)
        grad_embed, grad_first, grad_second = pullback(block_cot)
        return ((carry[0] + grad_first.astype(jnp.float32), carry[1] + grad_second.astype(jnp.float32)), (result, grad_embed))
    start = (jnp.zeros(w_in.shape, jnp.float32), jnp.zeros(w_out.shape, jnp.float32))
    (grad_w_in, grad_w_out), (outputs, embed_grad) = lax.scan(advance, start, (blocks, doc_ids, cotangents))
    per_lookup = jnp.broadcast_to(embed_grad.reshape(TOKENS, 1, D).astype(jnp.float32), (TOKENS, NTAB, D)).reshape(TOKENS * NTAB, D)
    grad_table = jax.ops.segment_sum(per_lookup, row_ids.reshape(-1), num_segments=ROWS)
    return (outputs.reshape(TOKENS, D), grad_w_in, grad_w_out, grad_table)
```

```python
import jax
import jax.numpy as jnp
from jax import lax
from jax.sharding import PartitionSpec as P

HEADS = 4
MAXLEN = 768


def normalize(values):
    center = values - jnp.mean(values, axis=-1, keepdims=True)
    spread = jnp.mean(center * center, axis=-1, keepdims=True)
    return center * lax.rsqrt(spread + 1e-06)


def hstu_layer(inputs, w_in, w_out, segment):
    length, width = inputs.shape
    head_dim = width // HEADS
    widened = inputs.astype(jnp.float32)
    normed = normalize(widened).astype(jnp.bfloat16)
    projected = jax.nn.silu(jnp.dot(normed, w_in, preferred_element_type=jnp.float32)).astype(
        jnp.bfloat16
    )
    gate_part, value_part, query_part, key_part = jnp.split(projected, 4, axis=1)
    query_heads = query_part.reshape(length, HEADS, head_dim)
    key_heads = key_part.reshape(length, HEADS, head_dim)
    value_heads = value_part.reshape(length, HEADS, head_dim)
    scores = jnp.einsum(
        "thd,shd->hts", query_heads, key_heads, preferred_element_type=jnp.float32
    ) * head_dim ** (-0.5)
    row_index = lax.broadcasted_iota(jnp.int32, (length, length), 0)
    col_index = lax.broadcasted_iota(jnp.int32, (length, length), 1)
    allowed = (segment[:, None] == segment[None, :]) & (row_index >= col_index)
    weights = (jnp.where(allowed[None], jax.nn.silu(scores), 0.0) / MAXLEN).astype(jnp.bfloat16)
    mixed = jnp.einsum(
        "hts,shd->thd", weights, value_heads, preferred_element_type=jnp.float32
    ).reshape(length, width)
    gated = (normalize(mixed) * gate_part.astype(jnp.float32)).astype(jnp.bfloat16)
    return (widened + jnp.dot(gated, w_out, preferred_element_type=jnp.float32)).astype(
        jnp.bfloat16
    )


def slot_onehot(place, capacity):
    events, owners = place.shape
    spots = lax.broadcasted_iota(jnp.int32, (events, owners, capacity), 2)
    return (place[:, :, None] == spots).astype(jnp.bfloat16).reshape(events, owners * capacity)


def shards(table, w_in, w_out, owner, local_row, doc_ids, out_grad):
    events, lookups_each = owner.shape
    width = table.shape[1]
    rows_owned = table.shape[0]
    owners = lax.axis_size("table")
    capacity = 2 * events * lookups_each // owners
    hits = owner[:, :, None] == jnp.arange(owners, dtype=jnp.int32)[None, None, :]
    member = jnp.sum(hits.astype(jnp.int32), axis=1)
    wanted = jnp.sum(jnp.where(hits, local_row[:, :, None], 0), axis=1)
    earlier = lax.broadcasted_iota(jnp.int32, (events, events), 0) > lax.broadcasted_iota(
        jnp.int32, (events, events), 1
    )
    before = jnp.dot(
        earlier.astype(jnp.bfloat16),
        member.astype(jnp.bfloat16),
        preferred_element_type=jnp.float32,
    ).astype(jnp.int32)
    place = jnp.where(member > 0, before, -1)
    spots = lax.broadcasted_iota(jnp.int32, (owners, capacity, events), 1)
    requests = jnp.sum(
        jnp.where(place.T[:, None, :] == spots, wanted.T[:, None, :], 0), axis=2
    )
    asked = lax.all_to_all(requests, "table", split_axis=0, concat_axis=0, tiled=True)
    asked_flat = asked.reshape(owners * capacity)
    rows = lax.broadcasted_iota(jnp.int32, (owners * capacity, rows_owned), 1)
    select = (asked_flat[:, None] == rows).astype(jnp.bfloat16)
    found = jnp.dot(select, table, preferred_element_type=jnp.float32).astype(jnp.bfloat16)
    arrived = lax.all_to_all(
        found.reshape(owners, capacity, width), "table", split_axis=0, concat_axis=0, tiled=True
    ).reshape(owners * capacity, width)
    embedded = jnp.dot(
        slot_onehot(place, capacity), arrived, preferred_element_type=jnp.float32
    ).astype(jnp.bfloat16)
    segment = doc_ids[0]

    def forward(first, second, third):
        return hstu_layer(first, second, third, segment)

    layer_out, pullback = jax.vjp(forward, embedded, w_in, w_out)
    embed_grad, grad_first, grad_second = lax.optimization_barrier(pullback(out_grad))
    grad_w_in, grad_w_out = lax.psum((grad_first, grad_second), ("dp", "table"))
    sending = lax.dot_general(
        slot_onehot(place, capacity),
        embed_grad,
        (((0,), (0,)), ((), ())),
        preferred_element_type=jnp.float32,
    ).astype(jnp.bfloat16)
    received = lax.all_to_all(
        sending.reshape(owners, capacity, width), "table", split_axis=0, concat_axis=0, tiled=True
    ).reshape(owners * capacity, width)
    lines = lax.broadcasted_iota(jnp.int32, (rows_owned, owners * capacity), 0)
    spread = (asked_flat[None, :] == lines).astype(jnp.bfloat16)
    summed = jnp.dot(spread, received, preferred_element_type=jnp.float32)
    grad_table = lax.psum_scatter(
        summed.astype(jnp.bfloat16), "dp", scatter_dimension=1, tiled=True
    ).astype(jnp.float32)
    return (
        layer_out,
        grad_w_in.astype(jnp.float32),
        grad_w_out.astype(jnp.float32),
        grad_table,
    )


def solution(mesh):
    placed = (
        P("table", None),
        P(),
        P(),
        P(("dp", "table"), None),
        P(("dp", "table"), None),
        P(("dp", "table"), None),
        P(("dp", "table"), None),
    )
    return jax.shard_map(
        shards,
        mesh=mesh,
        in_specs=placed,
        out_specs=(P(("dp", "table"), None), P(), P(), P("table", "dp")),
        check_vma=False,
    )
```

```python
import jax
import jax.numpy as jnp
from jax import lax
from jax.experimental import pallas as pl
from jax.experimental.pallas import tpu as pltpu
from jax.sharding import PartitionSpec as P

HEADS = 4
MAXLEN = 768


def normalize(values):
    center = values - jnp.mean(values, axis=-1, keepdims=True)
    spread = jnp.mean(center * center, axis=-1, keepdims=True)
    return center * lax.rsqrt(spread + 1e-06)


def hstu_layer(inputs, w_in, w_out, segment):
    length, width = inputs.shape
    head_dim = width // HEADS
    widened = inputs.astype(jnp.float32)
    normed = normalize(widened).astype(jnp.bfloat16)
    projected = jax.nn.silu(jnp.dot(normed, w_in, preferred_element_type=jnp.float32)).astype(
        jnp.bfloat16
    )
    gate_part, value_part, query_part, key_part = jnp.split(projected, 4, axis=1)
    query_heads = query_part.reshape(length, HEADS, head_dim)
    key_heads = key_part.reshape(length, HEADS, head_dim)
    value_heads = value_part.reshape(length, HEADS, head_dim)
    scores = jnp.einsum(
        "thd,shd->hts", query_heads, key_heads, preferred_element_type=jnp.float32
    ) * head_dim ** (-0.5)
    row_index = lax.broadcasted_iota(jnp.int32, (length, length), 0)
    col_index = lax.broadcasted_iota(jnp.int32, (length, length), 1)
    allowed = (segment[:, None] == segment[None, :]) & (row_index >= col_index)
    weights = (jnp.where(allowed[None], jax.nn.silu(scores), 0.0) / MAXLEN).astype(jnp.bfloat16)
    mixed = jnp.einsum(
        "hts,shd->thd", weights, value_heads, preferred_element_type=jnp.float32
    ).reshape(length, width)
    gated = (normalize(mixed) * gate_part.astype(jnp.float32)).astype(jnp.bfloat16)
    return (widened + jnp.dot(gated, w_out, preferred_element_type=jnp.float32)).astype(
        jnp.bfloat16
    )


def slot_onehot(place, capacity):
    events, owners = place.shape
    spots = lax.broadcasted_iota(jnp.int32, (events, owners, capacity), 2)
    return (place[:, :, None] == spots).astype(jnp.bfloat16).reshape(events, owners * capacity)


def pick_body(ids_ref, table_ref, out_ref):
    cells = lax.broadcasted_iota(jnp.int32, (ids_ref.shape[0], table_ref.shape[0]), 1)
    hit = (ids_ref[...] == cells).astype(jnp.bfloat16)
    out_ref[...] = jnp.dot(hit, table_ref[...], preferred_element_type=jnp.float32).astype(
        out_ref.dtype
    )


def add_body(ids_ref, values_ref, out_ref):
    parts, block, chunk = out_ref.shape
    first = pl.program_id(0) * block
    cells = first + lax.broadcasted_iota(jnp.int32, (block, values_ref.shape[0]), 0)
    hit = (ids_ref[...] == cells).astype(jnp.bfloat16)
    total = jnp.dot(hit, values_ref[...], preferred_element_type=jnp.float32)
    for part in range(parts):
        out_ref[part] = total[:, part * chunk : (part + 1) * chunk].astype(out_ref.dtype)


def block_of(size):
    return 256 if size % 256 == 0 else size


def pick_rows(ids, table):
    count, (rows, width) = ids.shape[0], table.shape
    block = block_of(count)
    return pl.pallas_call(
        pick_body,
        out_shape=jax.ShapeDtypeStruct((count, width), jnp.bfloat16),
        grid=(count // block,),
        in_specs=[
            pl.BlockSpec((block, 1), lambda i: (i, 0)),
            pl.BlockSpec((rows, width), lambda i: (0, 0)),
        ],
        out_specs=pl.BlockSpec((block, width), lambda i: (i, 0)),
        compiler_params=pltpu.CompilerParams(vmem_limit_bytes=40 * 1024 * 1024),
        cost_estimate=pl.CostEstimate(
            flops=2 * count * rows * width,
            bytes_accessed=2 * (count + rows) * width,
            transcendentals=0,
        ),
    )(ids.reshape(count, 1), table)


def add_rows(ids, values, rows, parts):
    count, width = values.shape
    block = block_of(rows)
    return pl.pallas_call(
        add_body,
        out_shape=jax.ShapeDtypeStruct((parts, rows, width // parts), jnp.bfloat16),
        grid=(rows // block,),
        in_specs=[
            pl.BlockSpec((1, count), lambda i: (0, 0)),
            pl.BlockSpec((count, width), lambda i: (0, 0)),
        ],
        out_specs=pl.BlockSpec((parts, block, width // parts), lambda i: (0, i, 0)),
        compiler_params=pltpu.CompilerParams(vmem_limit_bytes=40 * 1024 * 1024),
        cost_estimate=pl.CostEstimate(
            flops=2 * count * rows * width,
            bytes_accessed=2 * (count + rows) * width,
            transcendentals=0,
        ),
    )(ids.reshape(1, count), values)


def shards(table, w_in, w_out, owner, local_row, doc_ids, out_grad):
    events, lookups_each = owner.shape
    width = table.shape[1]
    rows_owned = table.shape[0]
    owners = lax.axis_size("table")
    capacity = 2 * events * lookups_each // owners
    hits = owner[:, :, None] == jnp.arange(owners, dtype=jnp.int32)[None, None, :]
    member = jnp.sum(hits.astype(jnp.int32), axis=1)
    wanted = jnp.sum(jnp.where(hits, local_row[:, :, None], 0), axis=1)
    earlier = lax.broadcasted_iota(jnp.int32, (events, events), 0) > lax.broadcasted_iota(
        jnp.int32, (events, events), 1
    )
    before = jnp.dot(
        earlier.astype(jnp.bfloat16),
        member.astype(jnp.bfloat16),
        preferred_element_type=jnp.float32,
    ).astype(jnp.int32)
    place = jnp.where(member > 0, before, -1)
    spots = lax.broadcasted_iota(jnp.int32, (owners, capacity, events), 1)
    requests = jnp.sum(
        jnp.where(place.T[:, None, :] == spots, wanted.T[:, None, :], 0), axis=2
    )
    asked = lax.all_to_all(requests, "table", split_axis=0, concat_axis=0, tiled=True)
    asked_flat = asked.reshape(owners * capacity)
    found = pick_rows(asked_flat, table)
    arrived = lax.all_to_all(
        found.reshape(owners, capacity, width), "table", split_axis=0, concat_axis=0, tiled=True
    ).reshape(owners * capacity, width)
    embedded = jnp.dot(
        slot_onehot(place, capacity), arrived, preferred_element_type=jnp.float32
    ).astype(jnp.bfloat16)
    segment = doc_ids[0]

    def forward(first, second, third):
        return hstu_layer(first, second, third, segment)

    layer_out, pullback = jax.vjp(forward, embedded, w_in, w_out)
    embed_grad, grad_first, grad_second = lax.optimization_barrier(pullback(out_grad))
    groups = lax.axis_size("dp")
    terms = jnp.concatenate([grad_first, grad_second], axis=1)
    partial_sum = lax.psum_scatter(terms, "dp", scatter_dimension=0, tiled=True)
    sending = lax.dot_general(
        slot_onehot(place, capacity),
        embed_grad,
        (((0,), (0,)), ((), ())),
        preferred_element_type=jnp.float32,
    ).astype(jnp.bfloat16)
    received = lax.all_to_all(
        sending.reshape(owners, capacity, width), "table", split_axis=0, concat_axis=0, tiled=True
    ).reshape(owners * capacity, width)
    partial_sum, received = lax.optimization_barrier((partial_sum, received))
    pieces = lax.all_to_all(
        partial_sum.reshape(owners, width // (groups * owners), -1),
        "table",
        split_axis=0,
        concat_axis=0,
        tiled=True,
    )
    piece = jnp.sum(pieces.astype(jnp.float32), axis=0).astype(jnp.bfloat16)
    column = lax.all_gather(piece, "dp", axis=0, tiled=False)
    whole = lax.all_gather(column, "table", axis=0, tiled=False)
    weight_grads = (
        jnp.swapaxes(whole, 0, 1).reshape(width, terms.shape[1]).astype(jnp.float32)
    )
    summed = add_rows(asked_flat, received, rows_owned, groups)
    grad_table = lax.psum_scatter(summed, "dp", scatter_dimension=0, tiled=True)[0].astype(
        jnp.float32
    )
    return (
        layer_out,
        weight_grads[:, : w_in.shape[1]],
        weight_grads[:, w_in.shape[1] :],
        grad_table,
    )


def solution(mesh):
    placed = (
        P("table", None),
        P(),
        P(),
        P(("dp", "table"), None),
        P(("dp", "table"), None),
        P(("dp", "table"), None),
        P(("dp", "table"), None),
    )
    return jax.shard_map(
        shards,
        mesh=mesh,
        in_specs=placed,
        out_specs=(P(("dp", "table"), None), P(), P(), P("table", "dp")),
        check_vma=False,
    )
```
